32 devices in a mesh: parts: 2 (over y), label: 16 (over z, x, core), doc: 1.
Axes of the slice: x: 2, y: 2, z: 4, core: 2. Of those that a mesh axis runs over, the one named last changes fastest.
Arguments:
- features: bfloat16 [4096, 768], P(('parts', 'label', 'doc')), parts along dimension 0, may hold values from -6 to 6
- w_encoder: bfloat16 [768, 768], P('label'), may hold values from -0.21875 to 0.21875
- norm_gain: float32 [768], replicated, may hold values from 0.25 to 1.75
- label_table: bfloat16 [128, 128, 768], P(('parts', 'label')), parts along dimension 0, may hold values from -0.21875 to 0.21875
- block_place: int32 [128], P('parts'), parts along dimension 0, may hold values from 0 to 63, as said below
- beams: int32 [4096, 2], P(('parts', 'label', 'doc')), parts along dimension 0, may hold values from -1 to 63, as said below
- positives: int32 [4096, 4], P(('parts', 'label', 'doc')), parts along dimension 0, may hold values from 0 to 8191
Outputs:
- doc_grad: bfloat16 [4096, 768], P(('parts', 'label', 'doc')), parts along dimension 0
- label_grad: float32 [128, 128, 768], P(('parts', 'label'), 'doc'), parts along dimension 0
The draws below stay inside these ranges and needn't reach their ends.
There are 2 independent parts, one for each index of `parts`. The reference program is written for one: setup_inputs(seed, part) draws one part's arguments, and reference() takes and returns one part's arrays. A program takes and returns all parts, laid end to end along the dimension named above; an argument that names none is the same for every part. Nothing has to cross between parts.
Inputs may be any that keep to these rules, and one draw needn't show every extreme that they name: `block_place`: A permutation: each block has its own row. `beams`: entries are block ids or -1 for padding. Among the beam slots of the 128 documents of one device (aligned blocks of rows), at most 8 name any one block; on some device every block held by some label shard is named by exactly 8 of them.
All inputs are finite; a program needn't handle non-finite values.
Results may differ from the reference program's by a relative error of at most 0.015.
Values may be sent and summed in bfloat16 or wider, within the bound.
A program may use at most 64 MiB of HBM per device.

```python
import jax
import jax.numpy as jnp
from jax import lax

D = 768
BLK = 128
BEAM = 2
POS = 4
BLK_DEV = 4
DOC_DEV = 128
DOCS = 2048
BLOCKS = 64


def shared_layout(key):
    return jax.random.permutation(jax.random.fold_in(key, 101), BLOCKS).astype(jnp.int32)


def shared_beams(key):
    layout = shared_layout(key)
    device_total = DOCS // DOC_DEV
    slot_total = DOC_DEV * BEAM
    half_rows = BLOCKS // 2
    capacity = max(2, 2 * slot_total // BLOCKS)
    share = capacity // 2
    pair_total = min(half_rows, slot_total // capacity)
    subkeys = jax.random.split(jax.random.fold_in(key, 202), 7)
    starts = BLK_DEV * jax.random.randint(subkeys[0], (device_total, 1), 0, max(1, half_rows // BLK_DEV)).astype(jnp.int32)
    lower_rows = (starts + jnp.arange(pair_total, dtype=jnp.int32)[None, :]) % half_rows
    hot_counts = jax.random.randint(subkeys[1], (device_total, 1), 0, pair_total + 1).astype(jnp.int32)
    fullest = jax.random.randint(subkeys[2], (), 0, device_total).astype(jnp.int32)
    device_ids = jnp.arange(device_total, dtype=jnp.int32)[:, None]
    hot_counts = jnp.where(device_ids == fullest, pair_total, hot_counts)
    pair_ranks = jax.vmap(lambda sub: jax.random.permutation(sub, pair_total))(jax.random.split(subkeys[3], device_total)).astype(jnp.int32)
    hot_pairs = pair_ranks < hot_counts
    upward = jax.random.randint(subkeys[4], (device_total, 1), 0, 2).astype(jnp.int32)
    slot_ids = jnp.arange(slot_total, dtype=jnp.int32)
    pair_of = jnp.minimum(slot_ids // capacity, pair_total - 1)
    within = slot_ids % capacity
    used = slot_ids < pair_total * capacity
    slot_lower = lower_rows[:, pair_of]
    slot_hot = hot_pairs[:, pair_of]
    side = jnp.where(slot_hot, upward, (within >= share).astype(jnp.int32)[None, :])
    rows = (slot_lower + side * half_rows).astype(jnp.int32)
    cool_pad = jnp.logical_not(slot_hot) & (jax.random.randint(subkeys[5], rows.shape, 0, 8) == 0)
    padded = cool_pad | jnp.logical_not(used)[None, :]
    shuffles = jax.vmap(lambda sub: jax.random.permutation(sub, slot_total))(jax.random.split(subkeys[6], device_total)).astype(jnp.int32)
    rows = jnp.take_along_axis(rows, shuffles, axis=1)
    padded = jnp.take_along_axis(padded, shuffles, axis=1)
    inverse = jnp.argsort(layout).astype(jnp.int32)
    block_ids = inverse[rows]
    return jnp.where(padded, -1, block_ids).reshape(DOCS, BEAM).astype(jnp.int32)


def draw_block_place(key, part):
    return shared_layout(key)


def draw_beams(key, part):
    return shared_beams(key)


def draw_positives(key, part):
    block_ids = shared_beams(key)
    key = jax.random.fold_in(key, 3)
    subkeys = jax.random.split(key, 3)
    picked = jax.random.randint(subkeys[0], (DOCS, POS), 0, BEAM).astype(jnp.int32)
    chosen = jnp.take_along_axis(block_ids, picked, axis=1)
    offset = jax.random.randint(subkeys[1], (DOCS, POS), 0, BLK).astype(jnp.int32)
    fallback = jax.random.randint(subkeys[2], (DOCS, POS), 0, BLOCKS * BLK).astype(jnp.int32)
    return jnp.where(chosen >= 0, chosen * BLK + offset, fallback).astype(jnp.int32)


def steps_of(key, dims, cuts, low, high):
    level = 1.0
    for dim, parts in cuts:
        draws = jax.random.uniform(jax.random.fold_in(jax.random.fold_in(key, 6), dim), (parts,), jnp.float32, low / len(cuts), high / len(cuts))
        level = level * jnp.repeat(jnp.exp(draws), dims[dim] // parts).reshape((-1,) + (1,) * (len(dims) - 1 - dim))
    return level


def scatter_about(stream_key, shape, deviation, bound, pieces=(), kind=jnp.bfloat16):
    loudness = steps_of(stream_key, shape, pieces, -0.22, 0.18) if pieces else 1.0
    drawn = jax.random.normal(stream_key, shape, jnp.float32) * deviation * loudness
    return jnp.minimum(jnp.maximum(drawn, -bound), bound).astype(kind)


def setup_inputs(seed: int = 0, part: int = 0) -> dict:
    splits = jax.random.split(jax.random.key(seed), 8)
    part_keys = jax.random.split(jax.random.fold_in(splits[7], part), 8)
    return {
        "features": scatter_about(part_keys[0], (DOCS, D), 1.0, 6.0, ((0, 16),)),
        "w_encoder": scatter_about(splits[1], (D, D), D ** -0.5, 0.21875, ((0, 16),)),
        "norm_gain": jnp.clip(1.0 + 0.15 * jax.random.normal(splits[2], (D,), jnp.float32), 0.25, 1.75),
        "label_table": scatter_about(part_keys[3], (BLOCKS, BLK, D), D ** -0.5, 0.21875, ((0, 16),)),
        "block_place": draw_block_place(jax.random.fold_in(jax.random.fold_in(splits[7], part), 71), part),
        "beams": draw_beams(jax.random.fold_in(jax.random.fold_in(splits[7], part), 71), part),
        "positives": draw_positives(jax.random.fold_in(jax.random.fold_in(splits[7], part), 71), part),
    }


hinge_weight = 0.125

def reference(features, w_encoder, norm_gain, label_table, block_place, beams, positives):
    encoded = jnp.dot(features, w_encoder, preferred_element_type=jnp.float32)
    scale_rows = lax.rsqrt(lax.optimization_barrier(jnp.mean(encoded * encoded, axis=-1, keepdims=True)) + 1e-06)
    embedded = (encoded * scale_rows * norm_gain.astype(jnp.float32)).astype(jnp.bfloat16)
    doc_block = 64
    step_count = DOCS // doc_block
    label_offsets = jnp.arange(BLK, dtype=jnp.int32)

    def advance(grads, index):
        begin = (index * doc_block).astype(jnp.int32)
        emb_rows = lax.dynamic_slice_in_dim(embedded, begin, doc_block, 0).astype(jnp.float32)
        beam_rows = lax.dynamic_slice_in_dim(beams, begin, doc_block, 0)
        wanted = lax.dynamic_slice_in_dim(positives, begin, doc_block, 0)
        present = beam_rows >= 0
        block_ids = jnp.where(present, beam_rows, 0).astype(jnp.int32)
        table_rows = block_place[block_ids].astype(jnp.int32)
        gathered = label_table[table_rows].astype(jnp.float32)
        scores = jnp.einsum('ikjd,id->ikj', gathered, emb_rows)
        label_ids = block_ids[:, :, None] * BLK + label_offsets[None, None, :]
        matched = jnp.any(label_ids[:, :, :, None] == wanted[:, None, None, :], axis=-1)
        signs = jnp.where(matched, 1.0, -1.0).astype(jnp.float32)
        raw_coef = jnp.where(present[:, :, None], -2.0 * hinge_weight * signs * jnp.maximum(0.0, 1.0 - signs * scores), 0.0)
        coef_low = lax.optimization_barrier(raw_coef.astype(jnp.bfloat16))
        coef = coef_low.astype(jnp.float32)
        slot_grad = jnp.einsum('ikj,ikjd->ikd', coef, gathered).astype(jnp.bfloat16)
        doc_rows = lax.optimization_barrier(jnp.sum(slot_grad.astype(jnp.float32), axis=1)).astype(jnp.bfloat16)
        contrib = coef[:, :, :, None] * emb_rows[:, None, None, :]
        grads = grads.at[table_rows.reshape(-1)].add(contrib.reshape(-1, BLK, D))
        return (grads, doc_rows)
    start_grads = jnp.zeros((BLOCKS, BLK, D), jnp.float32)
    label_grad, doc_parts = lax.scan(advance, start_grads, jnp.arange(step_count, dtype=jnp.int32))
    return (doc_parts.reshape(DOCS, D), label_grad)
```

```python
import functools

import jax
import jax.numpy as jnp
from jax import lax
from jax.experimental import pallas as pl
from jax.experimental.pallas import tpu as pltpu
from jax.sharding import PartitionSpec as P

hinge_weight = 0.125
BLOCK = 128


def coefficients(entry_emb, entry_info, table_blocks):
    label_span = table_blocks.shape[1]
    scores = jnp.einsum("bcd,bjd->bcj", entry_emb, table_blocks, preferred_element_type=jnp.float32)
    positions = jnp.arange(label_span, dtype=jnp.int32)
    matched = jnp.any(entry_info[:, :, 1:, None] == positions[None, None, None, :], axis=2)
    signs = jnp.where(matched, 1.0, -1.0).astype(jnp.float32)
    valid = entry_info[:, :, 0:1] > 0
    raw_coef = jnp.where(
        valid, -2.0 * hinge_weight * signs * jnp.maximum(0.0, 1.0 - signs * scores), 0.0
    )
    return raw_coef.astype(jnp.bfloat16)


def local(features, w_encoder, norm_gain, label_table, block_place, beams, positives):
    doc_total, width = features.shape
    blocks_here = label_table.shape[0]
    block_size = label_table.shape[1]
    label_shards = lax.axis_size("label")
    encoded = jnp.dot(
        features,
        lax.all_gather(w_encoder, "label", axis=0, tiled=True),
        preferred_element_type=jnp.float32,
    )
    scale_rows = lax.rsqrt(jnp.mean(encoded * encoded, axis=-1, keepdims=True) + 1e-06)
    embedded = (encoded * scale_rows * norm_gain).astype(jnp.bfloat16)
    beam_width = beams.shape[1]
    slot_total = doc_total * beam_width
    total_blocks = blocks_here * label_shards
    capacity = max(2, 2 * slot_total // total_blocks)
    buffer_size = total_blocks * capacity
    present = beams >= 0
    block_ids = jnp.where(present, beams, 0)
    table_rows = block_place[block_ids].reshape(-1)
    present_flat = present.reshape(-1)
    row_hits = (
        (table_rows[:, None] == jnp.arange(total_blocks, dtype=jnp.int32)[None, :])
        & present_flat[:, None]
    ).astype(jnp.int32)
    ranks = jnp.sum((jnp.cumsum(row_hits, axis=0) - row_hits) * row_hits, axis=1)
    slot_target = jnp.where(present_flat, table_rows * capacity + ranks, buffer_size)
    source_docs = (
        jnp.zeros((buffer_size,), jnp.int32)
        .at[slot_target]
        .set(jnp.arange(slot_total, dtype=jnp.int32) // beam_width, mode="drop")
    )
    occupied = jnp.zeros((buffer_size,), jnp.bool_).at[slot_target].set(True, mode="drop")
    outgoing = jnp.where(occupied[:, None], embedded[source_docs], jnp.zeros((), jnp.bfloat16))
    outgoing = outgoing.reshape(label_shards, blocks_here, capacity, width)
    offsets = positives[:, None, :] - block_ids[:, :, None] * block_size
    offsets = jnp.where(present[:, :, None] & (offsets >= 0) & (offsets < block_size), offsets, -1)
    slot_info = jnp.concatenate(
        [jnp.ones((slot_total, 1), jnp.int32), offsets.reshape(slot_total, -1)], axis=1
    )
    info_buffer = (
        jnp.zeros((buffer_size, slot_info.shape[1]), jnp.int32)
        .at[slot_target]
        .set(slot_info, mode="drop")
    )
    info_buffer = info_buffer.reshape(label_shards, blocks_here, capacity, -1)
    arrived, arrived_info = (
        lax.all_to_all(outgoing, "label", split_axis=0, concat_axis=2, tiled=True),
        lax.all_to_all(info_buffer, "label", split_axis=0, concat_axis=2, tiled=True),
    )
    entry_count = label_shards * capacity
    arrived = arrived.reshape(blocks_here, entry_count, width)
    arrived_info = arrived_info.reshape(blocks_here, entry_count, -1)
    coef = coefficients(arrived, arrived_info, label_table)
    replies = jnp.einsum(
        "bcj,bjd->bcd", coef, label_table, preferred_element_type=jnp.float32
    ).astype(jnp.bfloat16)
    returned = lax.all_to_all(
        replies.reshape(1, blocks_here, entry_count, width),
        "label",
        split_axis=2,
        concat_axis=0,
        tiled=True,
    )
    returned = returned.reshape(buffer_size, width)
    per_slot = jnp.where(
        present_flat[:, None],
        returned[jnp.minimum(slot_target, buffer_size - 1)],
        jnp.zeros((), jnp.bfloat16),
    )
    doc_grad = jnp.sum(
        per_slot.reshape(doc_total, beam_width, width).astype(jnp.float32), axis=1
    ).astype(jnp.bfloat16)
    partial_grad = jnp.einsum("bcj,bcd->bjd", coef, arrived, preferred_element_type=jnp.float32)
    label_grad = lax.psum_scatter(
        partial_grad.astype(jnp.bfloat16), "doc", scatter_dimension=1, tiled=True
    ).astype(jnp.float32)
    return (doc_grad, label_grad)


MESH = pl.DeviceIdType.MESH
META = 128


def flipped(index, mask):
    out = 0
    place = 1
    for _ in range(5):
        out = out + ((index // place) % 2 + (mask // place) % 2) % 2 * place
        place *= 2
    return out


def exchange_kernel(
    shards, capacity,
    feat_ref, w_ref, gain_ref, table_ref, place_ref, beams_ref, pos_ref,
    doc_ref, lab_ref,
    send_rows, arrived, w_all, embedded, coefs, replies, returned, pack,
    w_send, w_recv, relay_send, f_send, f_recv, r_send, r_recv,
):
    me = lax.axis_index("label")
    core = me % 2
    chip = me // 2
    partner = chip * 2 + 1 - core
    chips = shards // 2
    docs, width = feat_ref.shape
    piece = w_ref.shape[0]
    labels = table_ref.shape[0]
    blocks_here = labels // BLOCK
    slots = shards * capacity
    total_blocks = place_ref.shape[1]

    barrier = pltpu.get_barrier_semaphore()

    @pl.loop(1, shards)
    def _(t):
        pl.semaphore_signal(barrier, inc=1, device_id={"label": flipped(me, t)}, device_id_type=MESH)

    block_iota = lax.broadcasted_iota(jnp.int32, (docs, total_blocks), 1)
    place = place_ref[...]

    def row_of(block):
        return jnp.sum(jnp.where(block == block_iota, place + 1, 0), axis=1, keepdims=True)

    slot_iota = lax.broadcasted_iota(jnp.int32, (docs, slots), 1)
    slot_shard = slot_iota // capacity
    meta_iota = lax.broadcasted_iota(jnp.int32, (docs, META), 1)
    meta = jnp.zeros((docs, META), jnp.int32)
    hit = jnp.zeros((docs, slots), jnp.bool_)
    beam_width = beams_ref.shape[1]
    pos_total = pos_ref.shape[1]
    for k in range(beam_width):
        row = row_of(beams_ref[:, k : k + 1])
        meta = jnp.where(meta_iota == k, row, meta)
        target = jnp.where(row > 0, (row - 1) // blocks_here, -1)
        hit = hit | (target == slot_shard)
    for p in range(pos_total):
        wanted = pos_ref[:, p : p + 1]
        meta = jnp.where(meta_iota == beam_width + p, row_of(wanted // BLOCK), meta)
        meta = jnp.where(meta_iota == beam_width + pos_total + p, wanted % BLOCK, meta)
    hit_f = jnp.where(hit, 1.0, 0.0)
    above = (
        lax.broadcasted_iota(jnp.int32, (docs, docs), 0) > lax.broadcasted_iota(jnp.int32, (docs, docs), 1)
    )
    above = jnp.where(above, 1.0, 0.0).astype(jnp.bfloat16)
    rank = jnp.dot(above, hit_f.astype(jnp.bfloat16), preferred_element_type=jnp.float32)
    chosen = hit & (rank == (slot_iota % capacity).astype(jnp.float32))
    pack[...] = jnp.where(chosen, 1.0, 0.0).astype(jnp.bfloat16)
    over_docs = (((0,), (0,)), ((), ()))
    send_rows[:, :width] = lax.dot_general(
        pack[...], feat_ref[...], over_docs, preferred_element_type=jnp.float32
    ).astype(jnp.bfloat16)
    send_rows[:, width:] = lax.dot_general(
        pack[...], meta.astype(jnp.float32).astype(jnp.bfloat16), over_docs,
        preferred_element_type=jnp.float32,
    ).astype(jnp.bfloat16)

    def rows(index, size):
        return pl.ds(pl.multiple_of(index * size, size), size)

    def w_copy(owner, target, sem):
        return pltpu.make_async_remote_copy(
            src_ref=w_all.at[rows(owner, piece)], dst_ref=w_all.at[rows(owner, piece)],
            send_sem=sem, recv_sem=w_recv.at[owner],
            device_id={"label": target}, device_id_type=MESH,
        )

    def f_copy(target):
        return pltpu.make_async_remote_copy(
            src_ref=send_rows.at[rows(target, capacity)], dst_ref=arrived.at[rows(me, capacity)],
            send_sem=f_send.at[target], recv_sem=f_recv.at[me],
            device_id={"label": target}, device_id_type=MESH,
        )

    def f_arrival(source):
        return pltpu.make_async_remote_copy(
            src_ref=send_rows.at[rows(source, capacity)], dst_ref=arrived.at[rows(source, capacity)],
            send_sem=f_send.at[source], recv_sem=f_recv.at[source],
            device_id={"label": source}, device_id_type=MESH,
        )

    def r_copy(target):
        return pltpu.make_async_remote_copy(
            src_ref=replies.at[rows(target, capacity)], dst_ref=returned.at[rows(me, capacity)],
            send_sem=r_send.at[target], recv_sem=r_recv.at[me],
            device_id={"label": target}, device_id_type=MESH,
        )

    def r_arrival(source):
        return pltpu.make_async_remote_copy(
            src_ref=replies.at[rows(source, capacity)], dst_ref=returned.at[rows(source, capacity)],
            send_sem=r_send.at[source], recv_sem=r_recv.at[source],
            device_id={"label": source}, device_id_type=MESH,
        )

    w_all[rows(me, piece), :] = w_ref[...]
    arrived[rows(me, capacity), :] = send_rows[rows(me, capacity), :]
    pl.semaphore_wait(barrier, shards - 1)

    @pl.loop(0, chips - 1)
    def _(t):
        other = flipped(chip, chips - 1 - t)
        w_copy(me, other * 2 + core, w_send.at[other]).start()

    w_copy(me, partner, w_send.at[chip]).start()

    @pl.loop(0, shards - 1)
    def _(t):
        f_copy(flipped(me, shards - 1 - t)).start()

    @pl.loop(1, chips)
    def _(t):
        other = flipped(chip, t)
        owner = other * 2 + core
        w_copy(owner, partner, relay_send.at[other]).wait_recv()
        w_copy(owner, partner, relay_send.at[other]).start()

    @pl.loop(0, chips)
    def _(t):
        owner = flipped(chip, t) * 2 + 1 - core
        w_copy(owner, partner, w_send.at[chip]).wait_recv()

    group = 4
    chunk = group * capacity
    column = lax.broadcasted_iota(jnp.int32, (chunk, labels), 1)
    column_row = (column // BLOCK + me * blocks_here + 1).astype(jnp.float32)
    column_key = (column + (me * blocks_here + 1) * BLOCK).astype(jnp.float32)

    @pl.loop(0, shards // group)
    def _(t):
        plane = flipped(me // group, t)

        @pl.loop(0, group)
        def _(u):
            source = plane * group + u

            @pl.when(source != me)
            def _():
                f_arrival(source).wait_recv()

        here = rows(plane, chunk)
        encoded = jnp.dot(arrived[here, :width], w_all[...], preferred_element_type=jnp.float32)
        scale = lax.rsqrt(jnp.mean(encoded * encoded, axis=-1, keepdims=True) + 1e-06)
        emb = (encoded * scale * gain_ref[...]).astype(jnp.bfloat16)
        embedded[here, :] = emb
        info = arrived[here, width:].astype(jnp.float32)
        scores = lax.dot_general(
            emb, table_ref[...], (((1,), (1,)), ((), ())), preferred_element_type=jnp.float32
        )
        times = jnp.zeros((chunk, labels), jnp.float32)
        for k in range(beam_width):
            times = times + jnp.where(info[:, k : k + 1] == column_row, 1.0, 0.0)
        signs = jnp.full((chunk, labels), -1.0, jnp.float32)
        for p in range(pos_total):
            a, b = beam_width + p, beam_width + pos_total + p
            key = info[:, a : a + 1] * BLOCK + info[:, b : b + 1]
            signs = jnp.where(key == column_key, 1.0, signs)
        raw = -2.0 * hinge_weight * signs * jnp.maximum(0.0, 1.0 - signs * scores)
        coef = jnp.where(times > 0.0, raw, 0.0).astype(jnp.bfloat16) * times.astype(jnp.bfloat16)
        coefs[here, :] = coef
        replies[here, :] = jnp.dot(
            coef, table_ref[...], preferred_element_type=jnp.float32
        ).astype(jnp.bfloat16)

        @pl.loop(0, group)
        def _(u):
            source = plane * group + u

            @pl.when(source != me)
            def _():
                r_copy(source).start()

    returned[rows(me, capacity), :] = replies[rows(me, capacity), :]
    for b in range(blocks_here):
        lab_ref[b * BLOCK : (b + 1) * BLOCK, :] = lax.dot_general(
            coefs[:, b * BLOCK : (b + 1) * BLOCK], embedded[...], over_docs,
            preferred_element_type=jnp.float32,
        )

    @pl.loop(1, shards)
    def _(t):
        r_arrival(flipped(me, t)).wait_recv()

    doc_ref[...] = jnp.dot(
        pack[...], returned[...], preferred_element_type=jnp.float32
    ).astype(jnp.bfloat16)

    @pl.loop(1, shards)
    def _(t):
        other = flipped(me, t)
        f_copy(other).wait_send()
        r_copy(other).wait_send()

    @pl.loop(0, chips)
    def _(t):
        w_copy(me, partner, w_send.at[t]).wait_send()

    @pl.loop(1, chips)
    def _(t):
        w_copy(me, partner, relay_send.at[flipped(chip, t)]).wait_send()


def local_fused(features, w_encoder, norm_gain, label_table, block_place, beams, positives):
    docs, width = features.shape
    blocks_here, block_size, _ = label_table.shape
    shards = lax.axis_size("label")
    slot_total = docs * beams.shape[1]
    per_block = max(2, 2 * slot_total // (blocks_here * shards))
    capacity = blocks_here * per_block
    labels = blocks_here * block_size
    slots = shards * capacity
    vmem = pl.BlockSpec(memory_space=pltpu.VMEM)
    dma = pltpu.SemaphoreType.DMA
    doc_grad, label_grad = pl.pallas_call(
        functools.partial(exchange_kernel, shards, capacity),
        out_shape=(
            jax.ShapeDtypeStruct((docs, width), jnp.bfloat16),
            jax.ShapeDtypeStruct((labels, width), jnp.float32),
        ),
        in_specs=[vmem] * 7,
        out_specs=(vmem, vmem),
        scratch_shapes=[
            pltpu.VMEM((slots, width + META), jnp.bfloat16),
            pltpu.VMEM((slots, width + META), jnp.bfloat16),
            pltpu.VMEM((width, width), jnp.bfloat16),
            pltpu.VMEM((slots, width), jnp.bfloat16),
            pltpu.VMEM((slots, labels), jnp.bfloat16),
            pltpu.VMEM((slots, width), jnp.bfloat16),
            pltpu.VMEM((slots, width), jnp.bfloat16),
            pltpu.VMEM((docs, slots), jnp.bfloat16),
            dma((shards // 2,)), dma((shards,)), dma((shards // 2,)),
            dma((shards,)), dma((shards,)), dma((shards,)), dma((shards,)),
        ],
        compiler_params=pltpu.CompilerParams(
            collective_id=0, has_side_effects=True, vmem_limit_bytes=40 * 1024 * 1024
        ),
    )(
        features, w_encoder, norm_gain.reshape(1, width), label_table.reshape(labels, width),
        block_place.reshape(1, -1), beams, positives,
    )
    return doc_grad, label_grad.reshape(blocks_here, block_size, width)


def solution(mesh):
    placed = (
        P(("parts", "label", "doc"), None),
        P("label", None),
        P(),
        P(("parts", "label"), None, None),
        P("parts"),
        P(("parts", "label", "doc"), None),
        P(("parts", "label", "doc"), None),
    )
    one_kernel = mesh.shape["doc"] == 1 and mesh.shape["label"] == 16
    return jax.shard_map(
        local_fused if one_kernel else local,
        mesh=mesh,
        in_specs=placed,
        out_specs=(P(("parts", "label", "doc"), None), P(("parts", "label"), "doc", None)),
        check_vma=False,
    )
```

```python
import functools

import jax
import jax.numpy as jnp
from jax import lax
from jax.experimental import pallas as pl
from jax.experimental.pallas import tpu as pltpu
from jax.sharding import PartitionSpec as P

hinge_weight = 0.125
BLOCK = 128
LANES = 128


def coefficients(entry_emb, entry_info, table_blocks):
    label_span = table_blocks.shape[1]
    scores = jnp.einsum("bcd,bjd->bcj", entry_emb, table_blocks, preferred_element_type=jnp.float32)
    positions = jnp.arange(label_span, dtype=jnp.int32)
    matched = jnp.any(entry_info[:, :, 1:, None] == positions[None, None, None, :], axis=2)
    signs = jnp.where(matched, 1.0, -1.0).astype(jnp.float32)
    valid = entry_info[:, :, 0:1] > 0
    raw_coef = jnp.where(
        valid, -2.0 * hinge_weight * signs * jnp.maximum(0.0, 1.0 - signs * scores), 0.0
    )
    return raw_coef.astype(jnp.bfloat16)


def local(features, w_encoder, norm_gain, label_table, block_place, beams, positives):
    doc_total, width = features.shape
    blocks_here = label_table.shape[0]
    block_size = label_table.shape[1]
    label_shards = lax.axis_size("label")
    encoded = jnp.dot(
        features,
        lax.all_gather(w_encoder, "label", axis=0, tiled=True),
        preferred_element_type=jnp.float32,
    )
    scale_rows = lax.rsqrt(jnp.mean(encoded * encoded, axis=-1, keepdims=True) + 1e-06)
    embedded = (encoded * scale_rows * norm_gain).astype(jnp.bfloat16)
    beam_width = beams.shape[1]
    slot_total = doc_total * beam_width
    total_blocks = blocks_here * label_shards
    capacity = max(2, 2 * slot_total // total_blocks)
    buffer_size = total_blocks * capacity
    present = beams >= 0
    block_ids = jnp.where(present, beams, 0)
    table_rows = block_place[block_ids].reshape(-1)
    present_flat = present.reshape(-1)
    row_hits = (
        (table_rows[:, None] == jnp.arange(total_blocks, dtype=jnp.int32)[None, :])
        & present_flat[:, None]
    ).astype(jnp.int32)
    ranks = jnp.sum((jnp.cumsum(row_hits, axis=0) - row_hits) * row_hits, axis=1)
    slot_target = jnp.where(present_flat, table_rows * capacity + ranks, buffer_size)
    source_docs = (
        jnp.zeros((buffer_size,), jnp.int32)
        .at[slot_target]
        .set(jnp.arange(slot_total, dtype=jnp.int32) // beam_width, mode="drop")
    )
    occupied = jnp.zeros((buffer_size,), jnp.bool_).at[slot_target].set(True, mode="drop")
    outgoing = jnp.where(occupied[:, None], embedded[source_docs], jnp.zeros((), jnp.bfloat16))
    outgoing = outgoing.reshape(label_shards, blocks_here, capacity, width)
    offsets = positives[:, None, :] - block_ids[:, :, None] * block_size
    offsets = jnp.where(present[:, :, None] & (offsets >= 0) & (offsets < block_size), offsets, -1)
    slot_info = jnp.concatenate(
        [jnp.ones((slot_total, 1), jnp.int32), offsets.reshape(slot_total, -1)], axis=1
    )
    info_buffer = (
        jnp.zeros((buffer_size, slot_info.shape[1]), jnp.int32)
        .at[slot_target]
        .set(slot_info, mode="drop")
    )
    info_buffer = info_buffer.reshape(label_shards, blocks_here, capacity, -1)
    arrived, arrived_info = (
        lax.all_to_all(outgoing, "label", split_axis=0, concat_axis=2, tiled=True),
        lax.all_to_all(info_buffer, "label", split_axis=0, concat_axis=2, tiled=True),
    )
    entry_count = label_shards * capacity
    arrived = arrived.reshape(blocks_here, entry_count, width)
    arrived_info = arrived_info.reshape(blocks_here, entry_count, -1)
    coef = coefficients(arrived, arrived_info, label_table)
    replies = jnp.einsum(
        "bcj,bjd->bcd", coef, label_table, preferred_element_type=jnp.float32
    ).astype(jnp.bfloat16)
    returned = lax.all_to_all(
        replies.reshape(1, blocks_here, entry_count, width),
        "label",
        split_axis=2,
        concat_axis=0,
        tiled=True,
    )
    returned = returned.reshape(buffer_size, width)
    per_slot = jnp.where(
        present_flat[:, None],
        returned[jnp.minimum(slot_target, buffer_size - 1)],
        jnp.zeros((), jnp.bfloat16),
    )
    doc_grad = jnp.sum(
        per_slot.reshape(doc_total, beam_width, width).astype(jnp.float32), axis=1
    ).astype(jnp.bfloat16)
    partial_grad = jnp.einsum("bcj,bcd->bjd", coef, arrived, preferred_element_type=jnp.float32)
    label_grad = lax.psum_scatter(
        partial_grad.astype(jnp.bfloat16), "doc", scatter_dimension=1, tiled=True
    ).astype(jnp.float32)
    return (doc_grad, label_grad)


MESH = pl.DeviceIdType.MESH
META = 128


def flipped(index, mask):
    out = 0
    place = 1
    for _ in range(5):
        out = out + ((index // place) % 2 + (mask // place) % 2) % 2 * place
        place *= 2
    return out


def exchange_kernel(
    shards, capacity,
    feat_hbm, w_hbm, gain_hbm, table_hbm, place_hbm, beams_hbm, pos_hbm,
    doc_ref, lab_ref,
    feat_ref, gain_ref, table_ref, place_ref, beams_ref, pos_ref,
    send_rows, arrived, w_all, embedded, coefs, replies, returned, pack,
    load, wz_send, wx_send, wp_send, w_recv, f_send, f_recv, r_send, r_recv,
):
    me = lax.axis_index("label")
    core = me % 2
    cross = me // 2 % 2
    level = me // 4
    levels = shards // 4
    partner = me + 1 - 2 * core
    beside = me + 2 - 4 * cross
    docs, width = feat_ref.shape
    piece = w_hbm.shape[0]
    labels = table_ref.shape[0]
    blocks_here = labels // BLOCK
    slots = shards * capacity
    total_blocks = place_ref.shape[1]
    beam_width = beams_ref.shape[0]
    pos_total = pos_ref.shape[0]

    def rows(index, size):
        return pl.ds(pl.multiple_of(index * size, size), size)

    barrier = pltpu.get_barrier_semaphore()

    @pl.loop(1, shards)
    def _(t):
        pl.semaphore_signal(barrier, inc=1, device_id={"label": flipped(me, t)}, device_id_type=MESH)

    loads = [
        pltpu.make_async_copy(src, dst, load.at[i])
        for i, (src, dst) in enumerate((
            (beams_hbm, beams_ref), (place_hbm, place_ref), (pos_hbm, pos_ref), (feat_hbm, feat_ref),
            (w_hbm, w_all.at[rows(me, piece)]), (gain_hbm, gain_ref), (table_hbm, table_ref),
        ))
    ]
    for one in loads:
        one.start()
    for one in loads[:4]:
        one.wait()

    block_iota = lax.broadcasted_iota(jnp.int32, (total_blocks, docs), 0)
    place = (place_ref[...] + 1).astype(jnp.float32).astype(jnp.bfloat16)

    def row_of(block):
        at = jnp.where(block == block_iota, 1.0, 0.0).astype(jnp.bfloat16)
        return jnp.dot(place, at, preferred_element_type=jnp.float32).astype(jnp.int32)

    slot_iota = lax.broadcasted_iota(jnp.int32, (slots, docs), 0)
    slot_shard = slot_iota // capacity
    meta_iota = lax.broadcasted_iota(jnp.int32, (META, docs), 0)
    meta = jnp.zeros((META, docs), jnp.int32)
    hit = jnp.zeros((slots, docs), jnp.bool_)
    for k in range(beam_width):
        row = row_of(beams_ref[k : k + 1, :])
        meta = jnp.where(meta_iota == k, row, meta)
        target = jnp.where(row > 0, (row - 1) // blocks_here, -1)
        hit = hit | (target == slot_shard)
    for p in range(pos_total):
        wanted = pos_ref[p : p + 1, :]
        meta = jnp.where(meta_iota == beam_width + p, row_of(wanted // BLOCK), meta)
        meta = jnp.where(meta_iota == beam_width + pos_total + p, wanted % BLOCK, meta)
    hit_f = jnp.where(hit, 1.0, 0.0)
    before = (
        lax.broadcasted_iota(jnp.int32, (docs, docs), 0) < lax.broadcasted_iota(jnp.int32, (docs, docs), 1)
    )
    before = jnp.where(before, 1.0, 0.0).astype(jnp.bfloat16)
    rank = jnp.dot(hit_f.astype(jnp.bfloat16), before, preferred_element_type=jnp.float32)
    chosen = hit & (rank == (slot_iota % capacity).astype(jnp.float32))
    pack[...] = jnp.where(chosen, 1.0, 0.0).astype(jnp.bfloat16)
    over_docs = (((0,), (0,)), ((), ()))
    send_rows[:, :width] = jnp.dot(
        pack[...], feat_ref[...], preferred_element_type=jnp.float32
    ).astype(jnp.bfloat16)
    send_rows[:, width:] = lax.dot_general(
        pack[...], meta.astype(jnp.float32).astype(jnp.bfloat16), (((1,), (1,)), ((), ())),
        preferred_element_type=jnp.float32,
    ).astype(jnp.bfloat16)

    def w_copy(owner, target, sem):
        return pltpu.make_async_remote_copy(
            src_ref=w_all.at[rows(owner, piece)], dst_ref=w_all.at[rows(owner, piece)],
            send_sem=sem, recv_sem=w_recv.at[owner],
            device_id={"label": target}, device_id_type=MESH,
        )

    def slot_copy(out, into, send, recv, target, source):
        return pltpu.make_async_remote_copy(
            src_ref=out.at[rows(target, capacity)], dst_ref=into.at[rows(source, capacity)],
            send_sem=send.at[target], recv_sem=recv.at[source],
            device_id={"label": target}, device_id_type=MESH,
        )

    def f_copy(target):
        return slot_copy(send_rows, arrived, f_send, f_recv, target, me)

    def f_arrival(source):
        return slot_copy(send_rows, arrived, f_send, f_recv, source, source)

    def r_copy(target):
        return slot_copy(replies, returned, r_send, r_recv, target, me)

    def r_arrival(source):
        return slot_copy(replies, returned, r_send, r_recv, source, source)

    arrived[rows(me, capacity), :] = send_rows[rows(me, capacity), :]
    loads[4].wait()
    pl.semaphore_wait(barrier, shards - 1)

    same = cross * 2 + core

    def pass_on(z):
        w_copy(z * 4 + same, beside, wx_send.at[z]).start()
        w_copy(z * 4 + same, partner, wp_send.at[z * 2 + cross]).start()

    def features_to(t):
        plane = flipped(level, t)

        @pl.loop(0, 4)
        def _(u):
            target = plane * 4 + flipped(u, same)

            @pl.when(target != me)
            def _():
                f_copy(target).start()

    for s in range(levels):
        if s < levels - 1:
            @pl.when((level >= s) & (level < levels - 1))
            def _():
                if s:
                    w_copy(me - 4 * s, partner, wz_send.at[0]).wait_recv()
                w_copy(me - 4 * s, me + 4, wz_send.at[s]).start()

            @pl.when((level + s < levels) & (level > 0))
            def _():
                if s:
                    w_copy(me + 4 * s, partner, wz_send.at[0]).wait_recv()
                w_copy(me + 4 * s, me - 4, wz_send.at[levels + s]).start()

        if s:
            @pl.when((level >= s) & ((level == levels - 1) | (s == levels - 1)))
            def _():
                w_copy(me - 4 * s, partner, wz_send.at[0]).wait_recv()

            @pl.when((level + s < levels) & ((level == 0) | (s == levels - 1)))
            def _():
                w_copy(me + 4 * s, partner, wz_send.at[0]).wait_recv()

            @pl.when(level >= s)
            def _():
                pass_on(level - s)

            @pl.when(level + s < levels)
            def _():
                pass_on(level + s)
        else:
            pass_on(level)
        features_to(levels - 1 - s)

    @pl.loop(0, levels)
    def _(t):
        z = flipped(level, t)
        owner = z * 4 + (1 - cross) * 2 + core
        w_copy(owner, partner, wz_send.at[0]).wait_recv()
        w_copy(owner, partner, wp_send.at[z * 2 + 1 - cross]).start()

    @pl.loop(0, shards // 2)
    def _(t):
        w_copy(t * 2 + 1 - core, partner, wz_send.at[0]).wait_recv()

    loads[5].wait()
    loads[6].wait()
    gain = jnp.concatenate([gain_ref[i : i + 1, :] for i in range(width // LANES)], axis=1)
    group = 4
    chunk = group * capacity
    column = lax.broadcasted_iota(jnp.int32, (chunk, labels), 1)
    column_row = (column // BLOCK + me * blocks_here + 1).astype(jnp.float32)
    column_key = (column + (me * blocks_here + 1) * BLOCK).astype(jnp.float32)

    @pl.loop(0, shards // group)
    def _(t):
        plane = flipped(level, levels - 1 - t)

        @pl.loop(0, group)
        def _(u):
            source = plane * group + u

            @pl.when(source != me)
            def _():
                f_arrival(source).wait_recv()

        here = rows(plane, chunk)
        encoded = jnp.dot(arrived[here, :width], w_all[...], preferred_element_type=jnp.float32)
        scale = lax.rsqrt(jnp.mean(encoded * encoded, axis=-1, keepdims=True) + 1e-06)
        emb = (encoded * scale * gain).astype(jnp.bfloat16)
        embedded[here, :] = emb
        info = arrived[here, width:].astype(jnp.float32)
        scores = lax.dot_general(
            emb, table_ref[...], (((1,), (1,)), ((), ())), preferred_element_type=jnp.float32
        )
        times = jnp.zeros((chunk, labels), jnp.float32)
        for k in range(beam_width):
            times = times + jnp.where(info[:, k : k + 1] == column_row, 1.0, 0.0)
        signs = jnp.full((chunk, labels), -1.0, jnp.float32)
        for p in range(pos_total):
            a, b = beam_width + p, beam_width + pos_total + p
            key = info[:, a : a + 1] * BLOCK + info[:, b : b + 1]
            signs = jnp.where(key == column_key, 1.0, signs)
        raw = -2.0 * hinge_weight * signs * jnp.maximum(0.0, 1.0 - signs * scores)
        coef = jnp.where(times > 0.0, raw, 0.0).astype(jnp.bfloat16) * times.astype(jnp.bfloat16)
        coefs[here, :] = coef
        replies[here, :] = jnp.dot(
            coef, table_ref[...], preferred_element_type=jnp.float32
        ).astype(jnp.bfloat16)

        @pl.loop(0, group)
        def _(u):
            source = plane * group + u

            @pl.when(source != me)
            def _():
                r_copy(source).start()

    returned[rows(me, capacity), :] = replies[rows(me, capacity), :]
    for b in range(blocks_here):
        lab_ref[b * BLOCK : (b + 1) * BLOCK, :] = lax.dot_general(
            coefs[:, b * BLOCK : (b + 1) * BLOCK], embedded[...], over_docs,
            preferred_element_type=jnp.float32,
        )

    @pl.loop(1, shards)
    def _(t):
        r_arrival(flipped(me, t)).wait_recv()

    doc_ref[...] = lax.dot_general(
        pack[...], returned[...], over_docs, preferred_element_type=jnp.float32
    ).astype(jnp.bfloat16)

    @pl.loop(1, shards)
    def _(t):
        other = flipped(me, t)
        f_copy(other).wait_send()
        r_copy(other).wait_send()

    for s in range(levels - 1):
        @pl.when((level >= s) & (level < levels - 1))
        def _():
            w_copy(me, partner, wz_send.at[s]).wait_send()

        @pl.when((level + s < levels) & (level > 0))
        def _():
            w_copy(me, partner, wz_send.at[levels + s]).wait_send()

    @pl.loop(0, levels)
    def _(t):
        w_copy(me, partner, wx_send.at[t]).wait_send()

    @pl.loop(0, shards // 2)
    def _(t):
        w_copy(me, partner, wp_send.at[t]).wait_send()


def local_fused(features, w_encoder, norm_gain, label_table, block_place, beams, positives):
    docs, width = features.shape
    blocks_here, block_size, _ = label_table.shape
    shards = lax.axis_size("label")
    slot_total = docs * beams.shape[1]
    per_block = max(2, 2 * slot_total // (blocks_here * shards))
    capacity = blocks_here * per_block
    labels = blocks_here * block_size
    slots = shards * capacity
    vmem = pl.BlockSpec(memory_space=pltpu.VMEM)
    dma = pltpu.SemaphoreType.DMA
    doc_grad, label_grad = pl.pallas_call(
        functools.partial(exchange_kernel, shards, capacity),
        out_shape=(
            jax.ShapeDtypeStruct((docs, width), jnp.bfloat16),
            jax.ShapeDtypeStruct((labels, width), jnp.float32),
        ),
        in_specs=[pl.BlockSpec(memory_space=pl.ANY)] * 7,
        out_specs=(vmem, vmem),
        scratch_shapes=[
            pltpu.VMEM((docs, width), jnp.bfloat16),
            pltpu.VMEM((width // LANES, LANES), jnp.float32),
            pltpu.VMEM((labels, width), jnp.bfloat16),
            pltpu.VMEM((1, block_place.shape[0]), jnp.int32),
            pltpu.VMEM((beams.shape[1], docs), jnp.int32),
            pltpu.VMEM((positives.shape[1], docs), jnp.int32),
            pltpu.VMEM((slots, width + META), jnp.bfloat16),
            pltpu.VMEM((slots, width + META), jnp.bfloat16),
            pltpu.VMEM((width, width), jnp.bfloat16),
            pltpu.VMEM((slots, width), jnp.bfloat16),
            pltpu.VMEM((slots, labels), jnp.bfloat16),
            pltpu.VMEM((slots, width), jnp.bfloat16),
            pltpu.VMEM((slots, width), jnp.bfloat16),
            pltpu.VMEM((slots, docs), jnp.bfloat16),
            dma((7,)), dma((shards // 2,)), dma((shards // 4,)), dma((shards // 2,)), dma((shards,)),
            dma((shards,)), dma((shards,)), dma((shards,)), dma((shards,)),
        ],
        compiler_params=pltpu.CompilerParams(
            collective_id=0, has_side_effects=True, vmem_limit_bytes=60 * 1024 * 1024
        ),
    )(
        features, w_encoder, norm_gain.reshape(-1, LANES), label_table.reshape(labels, width),
        block_place.reshape(1, -1), beams.T, positives.T,
    )
    return doc_grad, label_grad.reshape(blocks_here, block_size, width)


def solution(mesh):
    placed = (
        P(("parts", "label", "doc"), None),
        P("label", None),
        P(),
        P(("parts", "label"), None, None),
        P("parts"),
        P(("parts", "label", "doc"), None),
        P(("parts", "label", "doc"), None),
    )
    one_kernel = mesh.shape["doc"] == 1 and mesh.shape["label"] == 16
    return jax.shard_map(
        local_fused if one_kernel else local,
        mesh=mesh,
        in_specs=placed,
        out_specs=(P(("parts", "label", "doc"), None), P(("parts", "label"), "doc", None)),
        check_vma=False,
    )
```

```python
import functools

import jax
import jax.numpy as jnp
from jax import lax
from jax.experimental import pallas as pl
from jax.experimental.pallas import tpu as pltpu
from jax.sharding import PartitionSpec as P

hinge_weight = 0.125
BLOCK = 128
LANES = 128


def coefficients(entry_emb, entry_info, table_blocks):
    label_span = table_blocks.shape[1]
    scores = jnp.einsum("bcd,bjd->bcj", entry_emb, table_blocks, preferred_element_type=jnp.float32)
    positions = jnp.arange(label_span, dtype=jnp.int32)
    matched = jnp.any(entry_info[:, :, 1:, None] == positions[None, None, None, :], axis=2)
    signs = jnp.where(matched, 1.0, -1.0).astype(jnp.float32)
    valid = entry_info[:, :, 0:1] > 0
    raw_coef = jnp.where(
        valid, -2.0 * hinge_weight * signs * jnp.maximum(0.0, 1.0 - signs * scores), 0.0
    )
    return raw_coef.astype(jnp.bfloat16)


def local(features, w_encoder, norm_gain, label_table, block_place, beams, positives):
    doc_total, width = features.shape
    blocks_here = label_table.shape[0]
    block_size = label_table.shape[1]
    label_shards = lax.axis_size("label")
    encoded = jnp.dot(
        features,
        lax.all_gather(w_encoder, "label", axis=0, tiled=True),
        preferred_element_type=jnp.float32,
    )
    scale_rows = lax.rsqrt(jnp.mean(encoded * encoded, axis=-1, keepdims=True) + 1e-06)
    embedded = (encoded * scale_rows * norm_gain).astype(jnp.bfloat16)
    beam_width = beams.shape[1]
    slot_total = doc_total * beam_width
    total_blocks = blocks_here * label_shards
    capacity = max(2, 2 * slot_total // total_blocks)
    buffer_size = total_blocks * capacity
    present = beams >= 0
    block_ids = jnp.where(present, beams, 0)
    table_rows = block_place[block_ids].reshape(-1)
    present_flat = present.reshape(-1)
    row_hits = (
        (table_rows[:, None] == jnp.arange(total_blocks, dtype=jnp.int32)[None, :])
        & present_flat[:, None]
    ).astype(jnp.int32)
    ranks = jnp.sum((jnp.cumsum(row_hits, axis=0) - row_hits) * row_hits, axis=1)
    slot_target = jnp.where(present_flat, table_rows * capacity + ranks, buffer_size)
    source_docs = (
        jnp.zeros((buffer_size,), jnp.int32)
        .at[slot_target]
        .set(jnp.arange(slot_total, dtype=jnp.int32) // beam_width, mode="drop")
    )
    occupied = jnp.zeros((buffer_size,), jnp.bool_).at[slot_target].set(True, mode="drop")
    outgoing = jnp.where(occupied[:, None], embedded[source_docs], jnp.zeros((), jnp.bfloat16))
    outgoing = outgoing.reshape(label_shards, blocks_here, capacity, width)
    offsets = positives[:, None, :] - block_ids[:, :, None] * block_size
    offsets = jnp.where(present[:, :, None] & (offsets >= 0) & (offsets < block_size), offsets, -1)
    slot_info = jnp.concatenate(
        [jnp.ones((slot_total, 1), jnp.int32), offsets.reshape(slot_total, -1)], axis=1
    )
    info_buffer = (
        jnp.zeros((buffer_size, slot_info.shape[1]), jnp.int32)
        .at[slot_target]
        .set(slot_info, mode="drop")
    )
    info_buffer = info_buffer.reshape(label_shards, blocks_here, capacity, -1)
    arrived, arrived_info = (
        lax.all_to_all(outgoing, "label", split_axis=0, concat_axis=2, tiled=True),
        lax.all_to_all(info_buffer, "label", split_axis=0, concat_axis=2, tiled=True),
    )
    entry_count = label_shards * capacity
    arrived = arrived.reshape(blocks_here, entry_count, width)
    arrived_info = arrived_info.reshape(blocks_here, entry_count, -1)
    coef = coefficients(arrived, arrived_info, label_table)
    replies = jnp.einsum(
        "bcj,bjd->bcd", coef, label_table, preferred_element_type=jnp.float32
    ).astype(jnp.bfloat16)
    returned = lax.all_to_all(
        replies.reshape(1, blocks_here, entry_count, width),
        "label",
        split_axis=2,
        concat_axis=0,
        tiled=True,
    )
    returned = returned.reshape(buffer_size, width)
    per_slot = jnp.where(
        present_flat[:, None],
        returned[jnp.minimum(slot_target, buffer_size - 1)],
        jnp.zeros((), jnp.bfloat16),
    )
    doc_grad = jnp.sum(
        per_slot.reshape(doc_total, beam_width, width).astype(jnp.float32), axis=1
    ).astype(jnp.bfloat16)
    partial_grad = jnp.einsum("bcj,bcd->bjd", coef, arrived, preferred_element_type=jnp.float32)
    label_grad = lax.psum_scatter(
        partial_grad.astype(jnp.bfloat16), "doc", scatter_dimension=1, tiled=True
    ).astype(jnp.float32)
    return (doc_grad, label_grad)


MESH = pl.DeviceIdType.MESH
META = 128


def flipped(index, mask):
    place = 1
    while place <= mask:
        if mask // place % 2:
            bit = lax.rem(lax.div(index, place), 2)
            index = index + (1 - 2 * bit) * place
        place *= 2
    return index


def exchange_kernel(
    shards, capacity,
    feat_hbm, w_hbm, gain_hbm, table_hbm, place_hbm, beams_hbm, pos_hbm,
    doc_ref, coefs, embedded,
    feat_ref, gain_ref, table_ref, place_ref, beams_ref, pos_ref,
    send_rows, arrived, w_all, replies, returned, pack,
    load, wz_send, wx_send, wp_send, w_recv, f_send, f_recv, r_send, r_recv,
):
    me = lax.axis_index("label")
    core = lax.rem(me, 2)
    cross = lax.rem(lax.div(me, 2), 2)
    level = lax.div(me, 4)
    levels = shards // 4
    partner = me + 1 - 2 * core
    beside = me + 2 - 4 * cross
    docs, width = feat_ref.shape
    piece = w_hbm.shape[0]
    labels = table_ref.shape[0]
    blocks_here = labels // BLOCK
    slots = shards * capacity
    total_blocks = place_ref.shape[1]
    beam_width = beams_ref.shape[0]
    pos_total = pos_ref.shape[0]

    def rows(index, size):
        return pl.ds(pl.multiple_of(index * size, size), size)

    barrier = pltpu.get_barrier_semaphore()

    @pl.loop(1, shards)
    def _(t):
        pl.semaphore_signal(barrier, inc=1, device_id={"label": lax.rem(me + t, shards)}, device_id_type=MESH)

    loads = [
        pltpu.make_async_copy(src, dst, load.at[i])
        for i, (src, dst) in enumerate((
            (beams_hbm, beams_ref), (place_hbm, place_ref), (pos_hbm, pos_ref), (feat_hbm, feat_ref),
            (w_hbm, w_all.at[rows(me, piece)]), (gain_hbm, gain_ref), (table_hbm, table_ref),
        ))
    ]
    for one in loads:
        one.start()
    def w_copy(owner, target, sem):
        return pltpu.make_async_remote_copy(
            src_ref=w_all.at[rows(owner, piece)], dst_ref=w_all.at[rows(owner, piece)],
            send_sem=sem, recv_sem=w_recv.at[owner],
            device_id={"label": target}, device_id_type=MESH,
        )

    def slot_copy(out, into, send, recv, target, source):
        return pltpu.make_async_remote_copy(
            src_ref=out.at[rows(target, capacity)], dst_ref=into.at[rows(source, capacity)],
            send_sem=send.at[target], recv_sem=recv.at[source],
            device_id={"label": target}, device_id_type=MESH,
        )

    def f_copy(target):
        return slot_copy(send_rows, arrived, f_send, f_recv, target, me)

    def f_arrival(source):
        return slot_copy(send_rows, arrived, f_send, f_recv, source, source)

    def r_copy(target):
        return slot_copy(replies, returned, r_send, r_recv, target, me)

    def r_arrival(source):
        return slot_copy(replies, returned, r_send, r_recv, source, source)

    same = cross * 2 + core

    def pass_on(z):
        w_copy(z * 4 + same, beside, wx_send.at[z]).start()
        w_copy(z * 4 + same, partner, wp_send.at[z * 2 + cross]).start()

    def features_to(t):
        plane = flipped(level, t)

        @pl.loop(0, 4)
        def _(u):
            target = plane * 4 + u

            @pl.when(target != me)
            def _():
                f_copy(target).start()

    loads[4].wait()
    pl.semaphore_wait(barrier, shards - 1)

    for t in range(1, levels):
        other = flipped(level, levels - t)
        w_copy(me, other * 4 + same, wz_send.at[other]).start()

    pass_on(level)

    for one in loads[:4]:
        one.wait()

    block_iota = lax.broadcasted_iota(jnp.int32, (total_blocks, docs), 0)
    place = (place_ref[...] + 1).astype(jnp.float32).astype(jnp.bfloat16)

    def row_of(block):
        at = jnp.where(block == block_iota, 1.0, 0.0).astype(jnp.bfloat16)
        return jnp.dot(place, at, preferred_element_type=jnp.float32).astype(jnp.int32)

    slot_iota = lax.broadcasted_iota(jnp.int32, (slots, docs), 0)
    slot_shard = slot_iota // capacity
    meta_iota = lax.broadcasted_iota(jnp.int32, (META, docs), 0)
    meta = jnp.zeros((META, docs), jnp.int32)
    hit = jnp.zeros((slots, docs), jnp.bool_)
    for k in range(beam_width):
        row = row_of(beams_ref[k : k + 1, :])
        meta = jnp.where(meta_iota == k, row, meta)
        target = jnp.where(row > 0, (row - 1) // blocks_here, -1)
        hit = hit | (target == slot_shard)
    for p in range(pos_total):
        wanted = pos_ref[p : p + 1, :]
        meta = jnp.where(meta_iota == beam_width + p, row_of(wanted // BLOCK), meta)
        meta = jnp.where(meta_iota == beam_width + pos_total + p, wanted % BLOCK, meta)
    hit_f = jnp.where(hit, 1.0, 0.0)
    before = (
        lax.broadcasted_iota(jnp.int32, (docs, docs), 0) < lax.broadcasted_iota(jnp.int32, (docs, docs), 1)
    )
    before = jnp.where(before, 1.0, 0.0).astype(jnp.bfloat16)
    rank = jnp.dot(hit_f.astype(jnp.bfloat16), before, preferred_element_type=jnp.float32)
    chosen = hit & (rank == (slot_iota % capacity).astype(jnp.float32))
    pack[...] = jnp.where(chosen, 1.0, 0.0).astype(jnp.bfloat16)
    over_docs = (((0,), (0,)), ((), ()))
    send_rows[:, :width] = jnp.dot(
        pack[...], feat_ref[...], preferred_element_type=jnp.float32
    ).astype(jnp.bfloat16)
    send_rows[:, width:] = lax.dot_general(
        pack[...], meta.astype(jnp.float32).astype(jnp.bfloat16), (((1,), (1,)), ((), ())),
        preferred_element_type=jnp.float32,
    ).astype(jnp.bfloat16)

    arrived[rows(me, capacity), :] = send_rows[rows(me, capacity), :]

    for t in (3, 2):
        features_to(t)

    for t in range(1, levels):
        z = flipped(level, t)
        w_copy(z * 4 + same, partner, wz_send.at[0]).wait_recv()
        pass_on(z)

    for t in range(0, levels):
        z = flipped(level, t)
        owner = z * 4 + (1 - cross) * 2 + core
        w_copy(owner, partner, wz_send.at[0]).wait_recv()
        w_copy(owner, partner, wp_send.at[z * 2 + 1 - cross]).start()

    for t in (1, 0):
        features_to(t)

    @pl.loop(0, shards // 2)
    def _(t):
        w_copy(t * 2 + 1 - core, partner, wz_send.at[0]).wait_recv()


    loads[5].wait()
    loads[6].wait()
    gain = jnp.concatenate([gain_ref[i : i + 1, :] for i in range(width // LANES)], axis=1)
    group = 4
    chunk = group * capacity
    column = lax.broadcasted_iota(jnp.int32, (chunk, labels), 1)
    column_row = (column // BLOCK + me * blocks_here + 1).astype(jnp.float32)
    column_key = (column + (me * blocks_here + 1) * BLOCK).astype(jnp.float32)

    @pl.loop(0, shards // group)
    def _(t):
        high, low = lax.div(level, 2), lax.rem(level, 2)
        plane = jnp.where(t < 2, 1 - high, high) * 2 + jnp.where(lax.rem(t, 2) == 0, 1 - low, low)

        @pl.loop(0, group)
        def _(u):
            source = plane * group + u

            @pl.when(source != me)
            def _():
                f_arrival(source).wait_recv()

        here = rows(plane, chunk)
        encoded = jnp.dot(arrived[here, :width], w_all[...], preferred_element_type=jnp.float32)
        scale = lax.rsqrt(jnp.mean(encoded * encoded, axis=-1, keepdims=True) + 1e-06)
        emb = (encoded * scale * gain).astype(jnp.bfloat16)
        embedded[here, :] = emb
        info = arrived[here, width:].astype(jnp.float32)
        scores = lax.dot_general(
            emb, table_ref[...], (((1,), (1,)), ((), ())), preferred_element_type=jnp.float32
        )
        times = jnp.zeros((chunk, labels), jnp.float32)
        for k in range(beam_width):
            times = times + jnp.where(info[:, k : k + 1] == column_row, 1.0, 0.0)
        signs = jnp.full((chunk, labels), -1.0, jnp.float32)
        for p in range(pos_total):
            a, b = beam_width + p, beam_width + pos_total + p
            key = info[:, a : a + 1] * BLOCK + info[:, b : b + 1]
            signs = jnp.where(key == column_key, 1.0, signs)
        raw = -2.0 * hinge_weight * signs * jnp.maximum(0.0, 1.0 - signs * scores)
        coef = jnp.where(times > 0.0, raw, 0.0).astype(jnp.bfloat16) * times.astype(jnp.bfloat16)
        coefs[here, :] = coef
        replies[here, :] = jnp.dot(
            coef, table_ref[...], preferred_element_type=jnp.float32
        ).astype(jnp.bfloat16)

        @pl.loop(0, group)
        def _(u):
            source = plane * group + u

            @pl.when(source != me)
            def _():
                r_copy(source).start()

    returned[rows(me, capacity), :] = replies[rows(me, capacity), :]
    @pl.loop(1, shards)
    def _(t):
        r_arrival(lax.rem(me + t, shards)).wait_recv()

    doc_ref[...] = lax.dot_general(
        pack[...], returned[...], over_docs, preferred_element_type=jnp.float32
    ).astype(jnp.bfloat16)

    @pl.loop(1, shards)
    def _(t):
        other = lax.rem(me + t, shards)
        f_copy(other).wait_send()
        r_copy(other).wait_send()

    for t in range(1, levels):
        w_copy(me, partner, wz_send.at[flipped(level, t)]).wait_send()

    for t in range(0, levels):
        w_copy(me, partner, wx_send.at[t]).wait_send()

    @pl.loop(0, shards // 2)
    def _(t):
        w_copy(me, partner, wp_send.at[t]).wait_send()


def local_fused(features, w_encoder, norm_gain, label_table, block_place, beams, positives):
    docs, width = features.shape
    blocks_here, block_size, _ = label_table.shape
    shards = lax.axis_size("label")
    slot_total = docs * beams.shape[1]
    per_block = max(2, 2 * slot_total // (blocks_here * shards))
    capacity = blocks_here * per_block
    labels = blocks_here * block_size
    slots = shards * capacity
    vmem = pl.BlockSpec(memory_space=pltpu.VMEM)
    dma = pltpu.SemaphoreType.DMA
    doc_grad, coefs, embedded = pl.pallas_call(
        functools.partial(exchange_kernel, shards, capacity),
        out_shape=(
            jax.ShapeDtypeStruct((docs, width), jnp.bfloat16),
            jax.ShapeDtypeStruct((slots, labels), jnp.bfloat16),
            jax.ShapeDtypeStruct((slots, width), jnp.bfloat16),
        ),
        in_specs=[pl.BlockSpec(memory_space=pl.ANY)] * 7,
        out_specs=(vmem, vmem, vmem),
        scratch_shapes=[
            pltpu.VMEM((docs, width), jnp.bfloat16),
            pltpu.VMEM((width // LANES, LANES), jnp.float32),
            pltpu.VMEM((labels, width), jnp.bfloat16),
            pltpu.VMEM((1, block_place.shape[0]), jnp.int32),
            pltpu.VMEM((beams.shape[1], docs), jnp.int32),
            pltpu.VMEM((positives.shape[1], docs), jnp.int32),
            pltpu.VMEM((slots, width + META), jnp.bfloat16),
            pltpu.VMEM((slots, width + META), jnp.bfloat16),
            pltpu.VMEM((width, width), jnp.bfloat16),
            pltpu.VMEM((slots, width), jnp.bfloat16),
            pltpu.VMEM((slots, width), jnp.bfloat16),
            pltpu.VMEM((slots, docs), jnp.bfloat16),
            dma((7,)), dma((shards // 2,)), dma((shards // 4,)), dma((shards // 2,)), dma((shards,)),
            dma((shards,)), dma((shards,)), dma((shards,)), dma((shards,)),
        ],
        compiler_params=pltpu.CompilerParams(
            collective_id=0, has_side_effects=True, vmem_limit_bytes=60 * 1024 * 1024
        ),
    )(
        features, w_encoder, norm_gain.reshape(-1, LANES), label_table.reshape(labels, width),
        block_place.reshape(1, -1), beams.T, positives.T,
    )
    label_grad = lax.dot_general(
        coefs, embedded, (((0,), (0,)), ((), ())), preferred_element_type=jnp.float32
    )
    return doc_grad, label_grad.reshape(blocks_here, block_size, width)


def solution(mesh):
    placed = (
        P(("parts", "label", "doc"), None),
        P("label", None),
        P(),
        P(("parts", "label"), None, None),
        P("parts"),
        P(("parts", "label", "doc"), None),
        P(("parts", "label", "doc"), None),
    )
    one_kernel = mesh.shape["doc"] == 1 and mesh.shape["label"] == 16
    return jax.shard_map(
        local_fused if one_kernel else local,
        mesh=mesh,
        in_specs=placed,
        out_specs=(P(("parts", "label", "doc"), None), P(("parts", "label"), "doc", None)),
        check_vma=False,
    )
```

```python
import functools

import jax
import jax.numpy as jnp
from jax import lax
from jax.experimental import pallas as pl
from jax.experimental.pallas import tpu as pltpu
from jax.sharding import PartitionSpec as P

hinge_weight = 0.125
BLOCK = 128
LANES = 128


def coefficients(entry_emb, entry_info, table_blocks):
    label_span = table_blocks.shape[1]
    scores = jnp.einsum("bcd,bjd->bcj", entry_emb, table_blocks, preferred_element_type=jnp.float32)
    positions = jnp.arange(label_span, dtype=jnp.int32)
    matched = jnp.any(entry_info[:, :, 1:, None] == positions[None, None, None, :], axis=2)
    signs = jnp.where(matched, 1.0, -1.0).astype(jnp.float32)
    valid = entry_info[:, :, 0:1] > 0
    raw_coef = jnp.where(
        valid, -2.0 * hinge_weight * signs * jnp.maximum(0.0, 1.0 - signs * scores), 0.0
    )
    return raw_coef.astype(jnp.bfloat16)


def local(features, w_encoder, norm_gain, label_table, block_place, beams, positives):
    doc_total, width = features.shape
    blocks_here = label_table.shape[0]
    block_size = label_table.shape[1]
    label_shards = lax.axis_size("label")
    encoded = jnp.dot(
        features,
        lax.all_gather(w_encoder, "label", axis=0, tiled=True),
        preferred_element_type=jnp.float32,
    )
    scale_rows = lax.rsqrt(jnp.mean(encoded * encoded, axis=-1, keepdims=True) + 1e-06)
    embedded = (encoded * scale_rows * norm_gain).astype(jnp.bfloat16)
    beam_width = beams.shape[1]
    slot_total = doc_total * beam_width
    total_blocks = blocks_here * label_shards
    capacity = max(2, 2 * slot_total // total_blocks)
    buffer_size = total_blocks * capacity
    present = beams >= 0
    block_ids = jnp.where(present, beams, 0)
    table_rows = block_place[block_ids].reshape(-1)
    present_flat = present.reshape(-1)
    row_hits = (
        (table_rows[:, None] == jnp.arange(total_blocks, dtype=jnp.int32)[None, :])
        & present_flat[:, None]
    ).astype(jnp.int32)
    ranks = jnp.sum((jnp.cumsum(row_hits, axis=0) - row_hits) * row_hits, axis=1)
    slot_target = jnp.where(present_flat, table_rows * capacity + ranks, buffer_size)
    source_docs = (
        jnp.zeros((buffer_size,), jnp.int32)
        .at[slot_target]
        .set(jnp.arange(slot_total, dtype=jnp.int32) // beam_width, mode="drop")
    )
    occupied = jnp.zeros((buffer_size,), jnp.bool_).at[slot_target].set(True, mode="drop")
    outgoing = jnp.where(occupied[:, None], embedded[source_docs], jnp.zeros((), jnp.bfloat16))
    outgoing = outgoing.reshape(label_shards, blocks_here, capacity, width)
    offsets = positives[:, None, :] - block_ids[:, :, None] * block_size
    offsets = jnp.where(present[:, :, None] & (offsets >= 0) & (offsets < block_size), offsets, -1)
    slot_info = jnp.concatenate(
        [jnp.ones((slot_total, 1), jnp.int32), offsets.reshape(slot_total, -1)], axis=1
    )
    info_buffer = (
        jnp.zeros((buffer_size, slot_info.shape[1]), jnp.int32)
        .at[slot_target]
        .set(slot_info, mode="drop")
    )
    info_buffer = info_buffer.reshape(label_shards, blocks_here, capacity, -1)
    arrived, arrived_info = (
        lax.all_to_all(outgoing, "label", split_axis=0, concat_axis=2, tiled=True),
        lax.all_to_all(info_buffer, "label", split_axis=0, concat_axis=2, tiled=True),
    )
    entry_count = label_shards * capacity
    arrived = arrived.reshape(blocks_here, entry_count, width)
    arrived_info = arrived_info.reshape(blocks_here, entry_count, -1)
    coef = coefficients(arrived, arrived_info, label_table)
    replies = jnp.einsum(
        "bcj,bjd->bcd", coef, label_table, preferred_element_type=jnp.float32
    ).astype(jnp.bfloat16)
    returned = lax.all_to_all(
        replies.reshape(1, blocks_here, entry_count, width),
        "label",
        split_axis=2,
        concat_axis=0,
        tiled=True,
    )
    returned = returned.reshape(buffer_size, width)
    per_slot = jnp.where(
        present_flat[:, None],
        returned[jnp.minimum(slot_target, buffer_size - 1)],
        jnp.zeros((), jnp.bfloat16),
    )
    doc_grad = jnp.sum(
        per_slot.reshape(doc_total, beam_width, width).astype(jnp.float32), axis=1
    ).astype(jnp.bfloat16)
    partial_grad = jnp.einsum("bcj,bcd->bjd", coef, arrived, preferred_element_type=jnp.float32)
    label_grad = lax.psum_scatter(
        partial_grad.astype(jnp.bfloat16), "doc", scatter_dimension=1, tiled=True
    ).astype(jnp.float32)
    return (doc_grad, label_grad)


MESH = pl.DeviceIdType.MESH
META = 16


def flipped(index, mask):
    place = 1
    while place <= mask:
        if mask // place % 2:
            bit = lax.rem(lax.div(index, place), 2)
            index = index + (1 - 2 * bit) * place
        place *= 2
    return index


def exchange_kernel(
    shards, capacity,
    feat_hbm, w_hbm, gain_hbm, table_hbm, place_hbm, beams_hbm, pos_hbm,
    doc_ref, coefs, embedded,
    feat_ref, gain_ref, table_ref, place_ref, beams_ref, pos_ref,
    send_rows, arrived, w_all, replies, returned, pack,
    load, wz_send, wx_send, wp_send, w_recv, f_send, f_recv, r_send, r_recv, m_send, m_recv, m_out, m_in,
):
    me = lax.axis_index("label")
    core = lax.rem(me, 2)
    cross = lax.rem(lax.div(me, 2), 2)
    level = lax.div(me, 4)
    levels = shards // 4
    partner = me + 1 - 2 * core
    beside = me + 2 - 4 * cross
    docs, width = feat_ref.shape
    piece = w_hbm.shape[0]
    labels = table_ref.shape[0]
    blocks_here = labels // BLOCK
    slots = shards * capacity
    total_blocks = place_ref.shape[1]
    beam_width = beams_ref.shape[0]
    pos_total = pos_ref.shape[0]

    def rows(index, size):
        return pl.ds(pl.multiple_of(index * size, size), size)

    barrier = pltpu.get_barrier_semaphore()

    @pl.loop(1, shards)
    def _(t):
        pl.semaphore_signal(barrier, inc=1, device_id={"label": lax.rem(me + t, shards)}, device_id_type=MESH)

    loads = [
        pltpu.make_async_copy(src, dst, load.at[i])
        for i, (src, dst) in enumerate((
            (beams_hbm, beams_ref), (place_hbm, place_ref), (pos_hbm, pos_ref), (feat_hbm, feat_ref),
            (w_hbm, w_all.at[rows(me, piece)]), (gain_hbm, gain_ref), (table_hbm, table_ref),
        ))
    ]
    for one in loads:
        one.start()
    def w_copy(owner, target, sem):
        return pltpu.make_async_remote_copy(
            src_ref=w_all.at[rows(owner, piece)], dst_ref=w_all.at[rows(owner, piece)],
            send_sem=sem, recv_sem=w_recv.at[owner],
            device_id={"label": target}, device_id_type=MESH,
        )

    def slot_copy(out, into, send, recv, target, source):
        return pltpu.make_async_remote_copy(
            src_ref=out.at[rows(target, capacity)], dst_ref=into.at[rows(source, capacity)],
            send_sem=send.at[target], recv_sem=recv.at[source],
            device_id={"label": target}, device_id_type=MESH,
        )

    def f_copy(target):
        return slot_copy(send_rows, arrived, f_send, f_recv, target, me)

    def f_arrival(source):
        return slot_copy(send_rows, arrived, f_send, f_recv, source, source)

    def m_copy(target, source):
        return pltpu.make_async_remote_copy(
            src_ref=m_out.at[rows(lax.div(target, 4), META)], dst_ref=m_in.at[rows(source, META)],
            send_sem=m_send.at[target], recv_sem=m_recv.at[source],
            device_id={"label": target}, device_id_type=MESH,
        )

    def r_copy(target):
        return slot_copy(replies, returned, r_send, r_recv, target, me)

    def r_arrival(source):
        return slot_copy(replies, returned, r_send, r_recv, source, source)

    same = cross * 2 + core

    def pass_on(z):
        w_copy(z * 4 + same, beside, wx_send.at[z]).start()
        w_copy(z * 4 + same, partner, wp_send.at[z * 2 + cross]).start()

    def features_to(t):
        plane = flipped(level, t)

        @pl.loop(0, 4)
        def _(u):
            target = plane * 4 + u

            @pl.when(target != me)
            def _():
                m_copy(target, me).start()
                f_copy(target).start()

    loads[4].wait()
    pl.semaphore_wait(barrier, shards - 1)

    for t in range(1, levels):
        other = flipped(level, levels - t)
        w_copy(me, other * 4 + same, wz_send.at[other]).start()

    pass_on(level)

    for one in loads[:4]:
        one.wait()

    block_iota = lax.broadcasted_iota(jnp.int32, (total_blocks, docs), 0)
    place = (place_ref[...] + 1).astype(jnp.float32).astype(jnp.bfloat16)

    def row_of(block):
        at = jnp.where(block == block_iota, 1.0, 0.0).astype(jnp.bfloat16)
        return jnp.dot(place, at, preferred_element_type=jnp.float32).astype(jnp.int32)

    slot_iota = lax.broadcasted_iota(jnp.int32, (slots, docs), 0)
    slot_shard = slot_iota // capacity
    meta_iota = lax.broadcasted_iota(jnp.int32, (META, docs), 0)
    meta = jnp.zeros((META, docs), jnp.int32)
    hit = jnp.zeros((slots, docs), jnp.bool_)
    for k in range(beam_width):
        row = row_of(beams_ref[k : k + 1, :])
        meta = jnp.where(meta_iota == k, row, meta)
        target = jnp.where(row > 0, (row - 1) // blocks_here, -1)
        hit = hit | (target == slot_shard)
    for p in range(pos_total):
        wanted = pos_ref[p : p + 1, :]
        meta = jnp.where(meta_iota == beam_width + p, row_of(wanted // BLOCK), meta)
        meta = jnp.where(meta_iota == beam_width + pos_total + p, wanted % BLOCK, meta)
    hit_f = jnp.where(hit, 1.0, 0.0)
    before = (
        lax.broadcasted_iota(jnp.int32, (docs, docs), 0) < lax.broadcasted_iota(jnp.int32, (docs, docs), 1)
    )
    before = jnp.where(before, 1.0, 0.0).astype(jnp.bfloat16)
    rank = jnp.dot(hit_f.astype(jnp.bfloat16), before, preferred_element_type=jnp.float32)
    chosen = hit & (rank == (slot_iota % capacity).astype(jnp.float32))
    pack[...] = jnp.where(chosen, 1.0, 0.0).astype(jnp.bfloat16)
    over_docs = (((0,), (0,)), ((), ()))
    send_rows[...] = jnp.dot(
        pack[...], feat_ref[...], preferred_element_type=jnp.float32
    ).astype(jnp.bfloat16)
    packed = lax.dot_general(
        meta.astype(jnp.float32).astype(jnp.bfloat16), pack[...], (((1,), (1,)), ((), ())),
        preferred_element_type=jnp.float32,
    ).astype(jnp.bfloat16)
    span = 4 * capacity
    for z in range(levels):
        m_out[z * META : (z + 1) * META, :] = packed[:, z * span : (z + 1) * span]
    m_in[rows(me, META), :] = m_out[rows(level, META), :]
    arrived[rows(me, capacity), :] = send_rows[rows(me, capacity), :]

    for t in (3, 2):
        features_to(t)

    for t in range(1, levels):
        z = flipped(level, t)
        w_copy(z * 4 + same, partner, wz_send.at[0]).wait_recv()
        pass_on(z)

    for t in range(0, levels):
        z = flipped(level, t)
        owner = z * 4 + (1 - cross) * 2 + core
        w_copy(owner, partner, wz_send.at[0]).wait_recv()
        w_copy(owner, partner, wp_send.at[z * 2 + 1 - cross]).start()

    for t in (1, 0):
        features_to(t)

    @pl.loop(0, shards // 2)
    def _(t):
        w_copy(t * 2 + 1 - core, partner, wz_send.at[0]).wait_recv()


    loads[5].wait()
    loads[6].wait()
    gain = jnp.concatenate([gain_ref[i : i + 1, :] for i in range(width // LANES)], axis=1)
    group = 4
    at = lax.broadcasted_iota(jnp.int32, (capacity, group * capacity), 1)
    own_slot = lax.broadcasted_iota(jnp.int32, (capacity, group * capacity), 0) + same * capacity
    mine = jnp.where(at == own_slot, 1.0, 0.0).astype(jnp.bfloat16)
    chunk = group * capacity
    column = lax.broadcasted_iota(jnp.int32, (chunk, labels), 1)
    column_row = (column // BLOCK + me * blocks_here + 1).astype(jnp.float32)
    column_key = (column + (me * blocks_here + 1) * BLOCK).astype(jnp.float32)

    @pl.loop(0, shards // group)
    def _(t):
        high, low = lax.div(level, 2), lax.rem(level, 2)
        plane = jnp.where(t < 2, 1 - high, high) * 2 + jnp.where(lax.rem(t, 2) == 0, 1 - low, low)

        @pl.loop(0, group)
        def _(u):
            source = plane * group + u

            @pl.when(source != me)
            def _():
                f_arrival(source).wait_recv()
                m_copy(source, source).wait_recv()

        here = rows(plane, chunk)
        encoded = jnp.dot(arrived[here, :], w_all[...], preferred_element_type=jnp.float32)
        scale = lax.rsqrt(jnp.mean(encoded * encoded, axis=-1, keepdims=True) + 1e-06)
        emb = (encoded * scale * gain).astype(jnp.bfloat16)
        embedded[here, :] = emb
        fields = lax.dot_general(
            mine, m_in[rows(plane, group * META), :], (((1,), (1,)), ((), ())),
            preferred_element_type=jnp.float32,
        )
        info = jnp.concatenate([fields[:, i * META : (i + 1) * META] for i in range(group)], axis=0)
        scores = lax.dot_general(
            emb, table_ref[...], (((1,), (1,)), ((), ())), preferred_element_type=jnp.float32
        )
        times = jnp.zeros((chunk, labels), jnp.float32)
        for k in range(beam_width):
            times = times + jnp.where(info[:, k : k + 1] == column_row, 1.0, 0.0)
        signs = jnp.full((chunk, labels), -1.0, jnp.float32)
        for p in range(pos_total):
            a, b = beam_width + p, beam_width + pos_total + p
            key = info[:, a : a + 1] * BLOCK + info[:, b : b + 1]
            signs = jnp.where(key == column_key, 1.0, signs)
        raw = -2.0 * hinge_weight * signs * jnp.maximum(0.0, 1.0 - signs * scores)
        coef = jnp.where(times > 0.0, raw, 0.0).astype(jnp.bfloat16) * times.astype(jnp.bfloat16)
        coefs[here, :] = coef
        replies[here, :] = jnp.dot(
            coef, table_ref[...], preferred_element_type=jnp.float32
        ).astype(jnp.bfloat16)

        @pl.loop(0, group)
        def _(u):
            source = plane * group + u

            @pl.when(source != me)
            def _():
                r_copy(source).start()

    returned[rows(me, capacity), :] = replies[rows(me, capacity), :]
    @pl.loop(1, shards)
    def _(t):
        r_arrival(lax.rem(me + t, shards)).wait_recv()

    doc_ref[...] = lax.dot_general(
        pack[...], returned[...], over_docs, preferred_element_type=jnp.float32
    ).astype(jnp.bfloat16)

    @pl.loop(1, shards)
    def _(t):
        other = lax.rem(me + t, shards)
        f_copy(other).wait_send()
        m_copy(other, me).wait_send()
        r_copy(other).wait_send()

    for t in range(1, levels):
        w_copy(me, partner, wz_send.at[flipped(level, t)]).wait_send()

    for t in range(0, levels):
        w_copy(me, partner, wx_send.at[t]).wait_send()

    @pl.loop(0, shards // 2)
    def _(t):
        w_copy(me, partner, wp_send.at[t]).wait_send()


def local_fused(features, w_encoder, norm_gain, label_table, block_place, beams, positives):
    docs, width = features.shape
    blocks_here, block_size, _ = label_table.shape
    shards = lax.axis_size("label")
    slot_total = docs * beams.shape[1]
    per_block = max(2, 2 * slot_total // (blocks_here * shards))
    capacity = blocks_here * per_block
    labels = blocks_here * block_size
    slots = shards * capacity
    vmem = pl.BlockSpec(memory_space=pltpu.VMEM)
    dma = pltpu.SemaphoreType.DMA
    doc_grad, coefs, embedded = pl.pallas_call(
        functools.partial(exchange_kernel, shards, capacity),
        out_shape=(
            jax.ShapeDtypeStruct((docs, width), jnp.bfloat16),
            jax.ShapeDtypeStruct((slots, labels), jnp.bfloat16),
            jax.ShapeDtypeStruct((slots, width), jnp.bfloat16),
        ),
        in_specs=[pl.BlockSpec(memory_space=pl.ANY)] * 7,
        out_specs=(vmem, vmem, vmem),
        scratch_shapes=[
            pltpu.VMEM((docs, width), jnp.bfloat16),
            pltpu.VMEM((width // LANES, LANES), jnp.float32),
            pltpu.VMEM((labels, width), jnp.bfloat16),
            pltpu.VMEM((1, block_place.shape[0]), jnp.int32),
            pltpu.VMEM((beams.shape[1], docs), jnp.int32),
            pltpu.VMEM((positives.shape[1], docs), jnp.int32),
            pltpu.VMEM((slots, width), jnp.bfloat16),
            pltpu.VMEM((slots, width), jnp.bfloat16),
            pltpu.VMEM((width, width), jnp.bfloat16),
            pltpu.VMEM((slots, width), jnp.bfloat16),
            pltpu.VMEM((slots, width), jnp.bfloat16),
            pltpu.VMEM((slots, docs), jnp.bfloat16),
            dma((7,)), dma((shards // 2,)), dma((shards // 4,)), dma((shards // 2,)), dma((shards,)),
            dma((shards,)), dma((shards,)), dma((shards,)), dma((shards,)), dma((shards,)), dma((shards,)),
            pltpu.VMEM((shards // 4 * META, LANES), jnp.bfloat16),
            pltpu.VMEM((shards * META, LANES), jnp.bfloat16),
        ],
        compiler_params=pltpu.CompilerParams(
            collective_id=0, has_side_effects=True, vmem_limit_bytes=60 * 1024 * 1024
        ),
    )(
        features, w_encoder, norm_gain.reshape(-1, LANES), label_table.reshape(labels, width),
        block_place.reshape(1, -1), beams.T, positives.T,
    )
    label_grad = lax.dot_general(
        coefs, embedded, (((0,), (0,)), ((), ())), preferred_element_type=jnp.float32
    )
    return doc_grad, label_grad.reshape(blocks_here, block_size, width)


def solution(mesh):
    placed = (
        P(("parts", "label", "doc"), None),
        P("label", None),
        P(),
        P(("parts", "label"), None, None),
        P("parts"),
        P(("parts", "label", "doc"), None),
        P(("parts", "label", "doc"), None),
    )
    one_kernel = mesh.shape["doc"] == 1 and mesh.shape["label"] == 16
    return jax.shard_map(
        local_fused if one_kernel else local,
        mesh=mesh,
        in_specs=placed,
        out_specs=(P(("parts", "label", "doc"), None), P(("parts", "label"), "doc", None)),
        check_vma=False,
    )
```
